512 devices in a mesh: blk: 32 (over z, core), row: 16 (over x, y).
Axes of the slice: x: 4, y: 4, z: 16, core: 2. Of those that a mesh axis runs over, the one named last changes fastest.
Arguments:
- load_cases: float32 [32, 1536, 512], P('blk', 'row'), may hold values from -6 to 6
- lower_factor: bfloat16 [32, 5, 1536, 1536], P('blk', None, 'row'), may hold values from -0.0390625 to 0.0390625
- upper_factor: bfloat16 [32, 5, 1536, 1536], P('blk', None, 'row'), may hold values from -0.0390625 to 0.0390625
- inverse: bfloat16 [32, 1536, 1536], P('blk', 'row'), may hold values from -2 to 2, as said below
Outputs:
- response: float32 [32, 1536, 512], P('blk', 'row')
The draws below stay inside these ranges and needn't reach their ends.
Inputs may be any that keep to these rules, and one draw needn't show every extreme that they name: `inverse`: each block has its diagonal entries between 0.4 and 2 and small off-diagonal entries.
All inputs are finite; a program needn't handle non-finite values.
Results may differ from the reference program's by a relative error of at most 0.0035.
Values may be sent and summed in bfloat16 or wider, within the bound.
A program may use at most 64 MiB of HBM per device.

```python
import math
import jax
import jax.numpy as jnp
from jax import lax

B = 1536
R = 512
NF = 32
LEVELS = 5


def draw_inverse(key, part):
    key = jax.random.fold_in(key, 11)
    key_diag, key_off = jax.random.split(key)
    row_index = lax.broadcasted_iota(jnp.int32, (NF, B, B), 1)
    col_index = lax.broadcasted_iota(jnp.int32, (NF, B, B), 2)
    on_diagonal = (row_index == col_index).astype(jnp.float32)
    coupling = jnp.clip(jax.random.normal(key_off, (NF, B, B), jnp.float32), -4.0, 4.0) * 0.5 * B ** (-0.5)
    scales = jnp.exp(jax.random.uniform(key_diag, (NF, B, B), jnp.float32, math.log(0.5), math.log(2.0)))
    return (on_diagonal * scales + (1.0 - on_diagonal) * coupling).astype(jnp.bfloat16)


def steps_of(key, shape, cuts, smallest, largest):
    loudness, own = 1.0, jax.random.fold_in(key, 6)
    for dim, blocks in cuts:
        heights = jnp.exp(jax.random.uniform(jax.random.fold_in(own, dim), (blocks,), jnp.float32, smallest / len(cuts), largest / len(cuts)))
        loudness = loudness * jnp.repeat(heights, shape[dim] // blocks).reshape([-1 if axis == dim else 1 for axis in range(len(shape))])
    return loudness


def gaussian(own_key, extent, deviation, limit, pieces=(), dtype=jnp.bfloat16):
    result = deviation * jax.random.normal(own_key, extent, jnp.float32)
    if pieces:
        result = result * steps_of(own_key, extent, pieces, -0.22, 0.18)
    return jnp.clip(result, -limit, limit).astype(dtype)


def setup_inputs(seed: int = 0) -> dict:
    key_list = jax.random.split(jax.random.key(seed), 5)
    load_cases = gaussian(key_list[0], (NF, B, R), 1.0, 6.0, ((0, 32), (1, 16)), jnp.float32)
    lower_factor = gaussian(key_list[1], (NF, LEVELS, B, B), (16 * B) ** -0.5, 0.0390625, ((0, 32), (2, 16)))
    upper_factor = gaussian(key_list[2], (NF, LEVELS, B, B), (16 * B) ** -0.5, 0.0390625, ((0, 32), (2, 16)))
    inverse = draw_inverse(jax.random.fold_in(key_list[4], 71), 0)
    return {"load_cases": load_cases, "lower_factor": lower_factor, "upper_factor": upper_factor, "inverse": inverse}


def apply_blocks(blocks, vectors):
    return jnp.einsum("fij,fjr->fir", blocks.astype(jnp.float32), vectors.astype(jnp.float32), precision=lax.Precision.HIGHEST)


def reference(load_cases, lower_factor, upper_factor, inverse):
    current = load_cases
    for level_index in range(LEVELS):
        distance = 2 ** level_index
        rounded = lax.optimization_barrier(current.astype(jnp.bfloat16))
        padding = jnp.zeros((distance, B, R), jnp.bfloat16)
        earlier = jnp.concatenate([padding, rounded[:NF - distance]], axis=0)
        later_rows = jnp.concatenate([rounded[distance:], padding], axis=0)
        current = current - apply_blocks(lower_factor[:, level_index], earlier) - apply_blocks(upper_factor[:, level_index], later_rows)
    final = lax.optimization_barrier(current.astype(jnp.bfloat16))
    return apply_blocks(inverse, final)
```

```python
import jax
import jax.numpy as jnp
from jax import lax
from jax.experimental import pallas as pl
from jax.experimental.pallas import tpu as pltpu
from jax.sharding import PartitionSpec as P

MESH = pl.DeviceIdType.MESH
LEVELS = 5
FRAMES = 32
SIDE = 4
ROWS = 96
WIDTH = 128
CHUNKS = 4
FUSED = (0, 1, 2)
LAST = LEVELS


def units(level):
    if level < LEVELS - 1:
        return [(2 * level, 2**level), (2 * level + 1, -(2**level))]
    if level == LEVELS - 1:
        return [(2 * level, FRAMES // 2)]
    return [(2 * LEVELS - 1, 0)]


def kernel(load, lower, upper, inverse, out, fac, inv, cur, own, gat, fac_sem, z_sem, a_sem, b_sem, far_sem, send_sem, last_sem):
    frame = lax.axis_index("blk")
    row = lax.axis_index("row")
    x, y = row // SIDE, row % SIDE

    def device(shift, dx, dy):
        return ((frame + shift + FRAMES) % FRAMES, ((x + dx) % SIDE) * SIDE + (y + dy) % SIDE)

    loads = [
        pltpu.make_async_copy(lower.at[0], fac.at[0], fac_sem.at[0]),
        pltpu.make_async_copy(upper.at[0], fac.at[1], fac_sem.at[1]),
        pltpu.make_async_copy(inverse.at[0], inv, fac_sem.at[2]),
    ]
    for copy in loads:
        copy.start()

    partners = {(0, d, 0) for d in range(1, SIDE)} | {(0, 0, d) for d in range(1, SIDE)}
    for level in range(LEVELS):
        for _, shift in units(level):
            partners.add((shift, 0, 0))
            if level in FUSED:
                for d in range(1, SIDE):
                    partners |= {(shift, d, 0), (shift, 0, d)}
    barrier = pltpu.get_barrier_semaphore()
    for partner in sorted(partners):
        pl.semaphore_signal(barrier, inc=1, device_id=device(*partner), device_id_type=MESH)

    def along(level, chunk, index):
        return index if level < LEVELS - 1 else chunk % 2

    def step(turn, d):
        return (d, 0) if turn == 0 else (0, d)

    def line(u, c, turn, at, first=0, count=SIDE):
        if turn == 0:
            return gat.at[u, c, pl.ds(first, count), at]
        return gat.at[u, c, at, pl.ds(first, count)]

    def send(src, dst, sem, recv, to):
        pltpu.make_async_remote_copy(src_ref=src, dst_ref=dst, send_sem=sem, recv_sem=recv, device_id=to, device_id_type=MESH).start()

    def wait(ref, sem):
        pltpu.make_async_copy(ref, ref, sem).wait()

    def begin(level, c):
        value = cur[c].astype(jnp.bfloat16)
        if level == LAST:
            u, _ = units(level)[0]
            turn = along(level, c, 0)
            gat[u, c, x, y] = value
            for d in (2, 1, 3):
                send(gat.at[u, c, x, y], gat.at[u, c, x, y], last_sem.at[c], a_sem.at[u, c], device(0, *step(turn, d)))
            return
        own[level, c] = value
        for i, (u, shift) in enumerate(units(level)):
            turn = along(level, c, i)
            if level in FUSED:
                for d in (2, 1, 3, 0):
                    send(own.at[level, c], gat.at[u, c, x, y], send_sem.at[level, c], a_sem.at[u, c], device(shift, *step(turn, d)))
            else:
                send(own.at[level, c], gat.at[u, c, x, y], send_sem.at[level, c], z_sem.at[u, c], device(shift, 0, 0))

    def spread(level, c):
        if level in FUSED or level == LAST:
            return
        for i, (u, _) in enumerate(units(level)):
            turn = along(level, c, i)
            wait(gat.at[u, c, x, y], z_sem.at[u, c])
            for d in (2, 1, 3):
                send(gat.at[u, c, x, y], gat.at[u, c, x, y], send_sem.at[level, c], a_sem.at[u, c], device(0, *step(turn, d)))

    def cross(level, c):
        for i, (u, _) in enumerate(units(level)):
            turn = along(level, c, i)
            at = y if turn == 0 else x
            wait(line(u, c, turn, at, 0, SIDE if level in FUSED else SIDE - 1), a_sem.at[u, c])
            for d in (1, SIDE - 1):
                block = line(u, c, turn, at)
                send(block, block, send_sem.at[level, c], b_sem.at[u, c], device(0, *step(1 - turn, d)))

    def relay(level, c):
        for i, (u, _) in enumerate(units(level)):
            turn = along(level, c, i)
            at = y if turn == 0 else x
            wait(line(u, c, turn, pl.ds(0, 2)), b_sem.at[u, c])
            for half, d in ((0, 1), (1, SIDE - 1)):
                block = line(u, c, turn, (at + SIDE - d) % SIDE, half * 2, 2)
                send(block, block, send_sem.at[level, c], far_sem.at[u, c], device(0, *step(1 - turn, d)))

    def product(block, u, c):
        return jnp.dot(block, gat[u, c].reshape(SIDE * SIDE * ROWS, WIDTH), preferred_element_type=jnp.float32)

    def finish(level, c):
        for i, (u, _) in enumerate(units(level)):
            turn = along(level, c, i)
            wait(line(u, c, turn, 0), far_sem.at[u, c])
        if level < LEVELS - 1:
            total = cur[c]
            (u, shift), (v, _) = units(level)
            total = total - jnp.where(frame >= shift, product(fac[0, level], u, c), 0.0)
            total = total - jnp.where(frame < FRAMES - shift, product(fac[1, level], v, c), 0.0)
            cur[c] = total
        elif level == LEVELS - 1:
            u, shift = units(level)[0]
            side = 1 - frame // shift
            cur[c] = cur[c] - product(fac[side, level], u, c)
        else:
            u, _ = units(level)[0]
            out[0, :, pl.ds(c * WIDTH, WIDTH)] = product(inv[...], u, c)

    for c in range(CHUNKS):
        cur[c] = load[0, :, pl.ds(c * WIDTH, WIDTH)]
    pl.semaphore_wait(barrier, len(partners))
    for c in range(CHUNKS):
        begin(0, c)
    for copy in loads:
        copy.wait()
    for level in range(LEVELS + 1):
        for c in range(CHUNKS):
            spread(level, c)
        for c in range(CHUNKS):
            cross(level, c)
        for c in range(CHUNKS):
            relay(level, c)
        for c in range(CHUNKS):
            finish(level, c)
            if level < LAST:
                begin(level + 1, c)
    for level in range(LEVELS + 1):
        for c in range(CHUNKS):
            u = units(level)[0][0]
            if level < LEVELS - 1:
                wait(gat.at[pl.ds(u, 2), c], send_sem.at[level, c])
            elif level == LEVELS - 1:
                wait(gat.at[u, c], send_sem.at[level, c])
            else:
                wait(gat.at[u, c, 0, pl.ds(0, SIDE - 1)], last_sem.at[c])
                wait(gat.at[u, c, pl.ds(0, SIDE - 1)], send_sem.at[level, c])


def per_device(load_cases, lower_factor, upper_factor, inverse):
    count = 2 * LEVELS
    return pl.pallas_call(
        kernel,
        out_shape=jax.ShapeDtypeStruct((1, ROWS, CHUNKS * WIDTH), jnp.float32),
        in_specs=[pl.BlockSpec(memory_space=pltpu.VMEM)] + [pl.BlockSpec(memory_space=pl.ANY)] * 3,
        out_specs=pl.BlockSpec(memory_space=pltpu.VMEM),
        scratch_shapes=[
            pltpu.VMEM((2, LEVELS, ROWS, SIDE * SIDE * ROWS), jnp.bfloat16),
            pltpu.VMEM((ROWS, SIDE * SIDE * ROWS), jnp.bfloat16),
            pltpu.VMEM((CHUNKS, ROWS, WIDTH), jnp.float32),
            pltpu.VMEM((LEVELS, CHUNKS, ROWS, WIDTH), jnp.bfloat16),
            pltpu.VMEM((count, CHUNKS, SIDE, SIDE, ROWS, WIDTH), jnp.bfloat16),
            pltpu.SemaphoreType.DMA((3,)),
            pltpu.SemaphoreType.DMA((count, CHUNKS)),
            pltpu.SemaphoreType.DMA((count, CHUNKS)),
            pltpu.SemaphoreType.DMA((count, CHUNKS)),
            pltpu.SemaphoreType.DMA((count, CHUNKS)),
            pltpu.SemaphoreType.DMA((LEVELS + 1, CHUNKS)),
            pltpu.SemaphoreType.DMA((CHUNKS,)),
        ],
        compiler_params=pltpu.CompilerParams(collective_id=0, has_side_effects=True, vmem_limit_bytes=48 * 2**20),
        cost_estimate=pl.CostEstimate(flops=1_660_000_000, bytes_accessed=3_700_000, transcendentals=0),
        name="hull_solve",
    )(load_cases, lower_factor, upper_factor, inverse)


def solution(mesh):
    return jax.shard_map(
        per_device,
        mesh=mesh,
        in_specs=(
            P("blk", "row", None),
            P("blk", None, "row", None),
            P("blk", None, "row", None),
            P("blk", "row", None),
        ),
        out_specs=P("blk", "row", None),
        check_vma=False,
    )
```

```python
import jax
import jax.numpy as jnp
from jax import lax
from jax.experimental import pallas as pl
from jax.experimental.pallas import tpu as pltpu
from jax.sharding import PartitionSpec as P

MESH = pl.DeviceIdType.MESH
LEVELS = 5
FRAMES = 32
SIDE = 4
ROWS = 96
WIDTH = 128
CHUNKS = 4
FUSED = (0, 1)
DIRECT = (4, 5)
SPLIT = True
ORDER = (
    1, 2, 0, 3, 1, 0, 3, 0, 1, 2, 0, 3, 2, 1, 0, 2, 1, 0, 3, 1, 2, 0, 3, 1, 0, 2, 1, 3, 0, 2, 1, 3,
    0, 2, 1, 3, 0, 2, 1, 3, 2, 0, 3, 2, 1, 0, 3, 1, 0, 1, 3, 2, 0, 3, 1, 2, 3, 2, 0, 3, 1, 2, 0, 1,
    3, 0, 2, 1, 3, 2, 1, 3, 0, 2, 3, 1, 2, 0, 3, 2,
)
LAST = LEVELS


def units(level):
    if level < LEVELS - 1:
        return [(2 * level, 2**level), (2 * level + 1, -(2**level))]
    if level == LEVELS - 1:
        return [(2 * level, FRAMES // 2)]
    return [(2 * LEVELS - 1, 0)]


def kernel(load, lower, upper, inverse, out, whole, fac, inv, cur, own, gat, fac_sem, z_sem, a_sem, b_sem, far_sem, send_sem, last_sem):
    frame = lax.axis_index("blk")
    row = lax.axis_index("row")
    x, y = row // SIDE, row % SIDE

    def device(shift, dx, dy):
        return ((frame + shift + FRAMES) % FRAMES, ((x + dx) % SIDE) * SIDE + (y + dy) % SIDE)

    first = pltpu.make_async_copy(load.at[0], whole, fac_sem.at[3])
    first.start()
    loads = [
        pltpu.make_async_copy(lower.at[0], fac.at[0], fac_sem.at[0]),
        pltpu.make_async_copy(upper.at[0], fac.at[1], fac_sem.at[1]),
        pltpu.make_async_copy(inverse.at[0], inv, fac_sem.at[2]),
    ]
    for copy in loads:
        copy.start()

    partners = {(0, d, 0) for d in range(1, SIDE)} | {(0, 0, d) for d in range(1, SIDE)}
    for level in range(LEVELS):
        for _, shift in units(level):
            partners.add((shift, 0, 0))
            if level in FUSED:
                for d in range(1, SIDE):
                    partners |= {(shift, d, 0), (shift, 0, d)}
    barrier = pltpu.get_barrier_semaphore()
    for partner in sorted(partners):
        pl.semaphore_signal(barrier, inc=1, device_id=device(*partner), device_id_type=MESH)

    def along(level, chunk, index):
        return index if level < LEVELS - 1 else chunk % 2

    def step(turn, d):
        return (d, 0) if turn == 0 else (0, d)

    def line(u, c, turn, at, first=0, count=SIDE):
        if turn == 0:
            return gat.at[u, c, pl.ds(first, count), at]
        return gat.at[u, c, at, pl.ds(first, count)]

    def send(src, dst, sem, recv, to):
        pltpu.make_async_remote_copy(src_ref=src, dst_ref=dst, send_sem=sem, recv_sem=recv, device_id=to, device_id_type=MESH).start()

    def wait(ref, sem):
        pltpu.make_async_copy(ref, ref, sem).wait()

    def begin(level, c):
        value = cur[c].astype(jnp.bfloat16)
        if level == LAST:
            u, _ = units(level)[0]
            turn = along(level, c, 0)
            gat[u, c, x, y] = value
            for d in (2, 1, 3):
                send(gat.at[u, c, x, y], gat.at[u, c, x, y], last_sem.at[c], a_sem.at[u, c], device(0, *step(turn, d)))
            return
        own[level, c] = value
        for i, (u, shift) in enumerate(units(level)):
            turn = along(level, c, i)
            if level in FUSED:
                for d in (2, 1, 3, 0):
                    send(own.at[level, c], gat.at[u, c, x, y], send_sem.at[level, c], a_sem.at[u, c], device(shift, *step(turn, d)))
            else:
                send(own.at[level, c], gat.at[u, c, x, y], send_sem.at[level, c], z_sem.at[u, c], device(shift, 0, 0))

    def spread(level, c):
        for i, (u, _) in enumerate(units(level)):
            turn = along(level, c, i)
            wait(gat.at[u, c, x, y], z_sem.at[u, c])
            for d in (2, 1, 3):
                send(gat.at[u, c, x, y], gat.at[u, c, x, y], send_sem.at[level, c], a_sem.at[u, c], device(0, *step(turn, d)))

    def cross(level, c):
        for i, (u, _) in enumerate(units(level)):
            turn = along(level, c, i)
            at = y if turn == 0 else x
            wait(line(u, c, turn, at, 0, SIDE if level in FUSED else SIDE - 1), a_sem.at[u, c])
            if level in DIRECT:
                for d in (2, 1, 3):
                    block = line(u, c, turn, at)
                    send(block, block, send_sem.at[level, c], far_sem.at[u, c], device(0, *step(1 - turn, d)))
            elif SPLIT:
                for sems, first in ((b_sem, 0), (far_sem, 2)):
                    for d, half in ((1, first), (SIDE - 1, 2 - first)):
                        block = line(u, c, turn, at, half, 2)
                        send(block, block, send_sem.at[level, c], sems.at[u, c], device(0, *step(1 - turn, d)))
            else:
                for d in (1, SIDE - 1):
                    block = line(u, c, turn, at)
                    send(block, block, send_sem.at[level, c], b_sem.at[u, c], device(0, *step(1 - turn, d)))

    def relay(level, c):
        for i, (u, _) in enumerate(units(level)):
            turn = along(level, c, i)
            at = y if turn == 0 else x
            wait(line(u, c, turn, 0 if SPLIT else pl.ds(0, 2)), b_sem.at[u, c])
            for half, d in ((0, 1), (2, SIDE - 1)):
                block = line(u, c, turn, (at + SIDE - d) % SIDE, half, 2)
                send(block, block, send_sem.at[level, c], far_sem.at[u, c], device(0, *step(1 - turn, d)))

    def product(block, u, c):
        return jnp.dot(block, gat[u, c].reshape(SIDE * SIDE * ROWS, WIDTH), preferred_element_type=jnp.float32)

    def close(level, c):
        for i, (u, _) in enumerate(units(level)):
            turn = along(level, c, i)
            blocks = 3 if level in DIRECT else 2 if SPLIT else 1
            wait(line(u, c, turn, pl.ds(0, blocks)), far_sem.at[u, c])
        if level < LEVELS - 1:
            total = cur[c]
            (u, shift), (v, _) = units(level)
            total = total - jnp.where(frame >= shift, product(fac[0, level], u, c), 0.0)
            total = total - jnp.where(frame < FRAMES - shift, product(fac[1, level], v, c), 0.0)
            cur[c] = total
        elif level == LEVELS - 1:
            u, shift = units(level)[0]
            side = 1 - frame // shift
            cur[c] = cur[c] - product(fac[side, level], u, c)
        else:
            u, _ = units(level)[0]
            out[0, :, pl.ds(c * WIDTH, WIDTH)] = product(inv[...], u, c)
        if level < LAST:
            begin(level + 1, c)

    steps = [(begin, 0)]
    for level in range(LEVELS + 1):
        if level not in FUSED and level != LAST:
            steps.append((spread, level))
        steps.append((cross, level))
        if level not in DIRECT:
            steps.append((relay, level))
        steps.append((close, level))

    first.wait()
    for c in range(CHUNKS):
        cur[c] = whole[:, pl.ds(c * WIDTH, WIDTH)]
    for copy in loads:
        copy.wait()
    pl.semaphore_wait(barrier, len(partners))
    todo = [iter(steps) for _ in range(CHUNKS)]
    for c in ORDER:
        act, level = next(todo[c])
        act(level, c)
    for level in range(LEVELS + 1):
        for c in range(CHUNKS):
            u = units(level)[0][0]
            if level < LEVELS - 1:
                wait(gat.at[pl.ds(u, 2), c], send_sem.at[level, c])
            elif level == LEVELS - 1:
                wait(gat.at[u, c], send_sem.at[level, c])
            else:
                wait(gat.at[u, c, 0, pl.ds(0, SIDE - 1)], last_sem.at[c])
                wait(gat.at[u, c, pl.ds(0, SIDE - 1)], send_sem.at[level, c])


def per_device(load_cases, lower_factor, upper_factor, inverse):
    count = 2 * LEVELS
    return pl.pallas_call(
        kernel,
        out_shape=jax.ShapeDtypeStruct((1, ROWS, CHUNKS * WIDTH), jnp.float32),
        in_specs=[pl.BlockSpec(memory_space=pl.ANY)] * 4,
        out_specs=pl.BlockSpec(memory_space=pltpu.VMEM),
        scratch_shapes=[
            pltpu.VMEM((ROWS, CHUNKS * WIDTH), jnp.float32),
            pltpu.VMEM((2, LEVELS, ROWS, SIDE * SIDE * ROWS), jnp.bfloat16),
            pltpu.VMEM((ROWS, SIDE * SIDE * ROWS), jnp.bfloat16),
            pltpu.VMEM((CHUNKS, ROWS, WIDTH), jnp.float32),
            pltpu.VMEM((LEVELS, CHUNKS, ROWS, WIDTH), jnp.bfloat16),
            pltpu.VMEM((count, CHUNKS, SIDE, SIDE, ROWS, WIDTH), jnp.bfloat16),
            pltpu.SemaphoreType.DMA((4,)),
            pltpu.SemaphoreType.DMA((count, CHUNKS)),
            pltpu.SemaphoreType.DMA((count, CHUNKS)),
            pltpu.SemaphoreType.DMA((count, CHUNKS)),
            pltpu.SemaphoreType.DMA((count, CHUNKS)),
            pltpu.SemaphoreType.DMA((LEVELS + 1, CHUNKS)),
            pltpu.SemaphoreType.DMA((CHUNKS,)),
        ],
        compiler_params=pltpu.CompilerParams(collective_id=0, has_side_effects=True, vmem_limit_bytes=62 * 2**20),
        cost_estimate=pl.CostEstimate(flops=1_660_000_000, bytes_accessed=3_700_000, transcendentals=0),
        name="hull_solve",
    )(load_cases, lower_factor, upper_factor, inverse)


def solution(mesh):
    return jax.shard_map(
        per_device,
        mesh=mesh,
        in_specs=(
            P("blk", "row", None),
            P("blk", None, "row", None),
            P("blk", None, "row", None),
            P("blk", "row", None),
        ),
        out_specs=P("blk", "row", None),
        check_vma=False,
    )
```

```python
import jax
import jax.numpy as jnp
from jax import lax
from jax.experimental import pallas as pl
from jax.experimental.pallas import tpu as pltpu
from jax.sharding import PartitionSpec as P

MESH = pl.DeviceIdType.MESH
LEVELS = 5
FRAMES = 32
SIDE = 4
ROWS = 96
WIDTH = 128
CHUNKS = 4
FUSED = (0, 1)
DIRECT = (4, 5)
SPLIT = True
ORDER = (
    1, 2, 0, 3, 1, 0, 3, 0, 1, 2, 0, 3, 2, 1, 0, 2, 1, 0, 3, 1, 2, 0, 3, 1, 0, 2, 1, 3, 0, 2, 1, 3,
    0, 2, 1, 3, 0, 2, 1, 3, 2, 0, 3, 2, 1, 0, 3, 1, 0, 1, 3, 2, 0, 3, 1, 2, 3, 2, 0, 3, 1, 2, 0, 1,
    3, 0, 2, 1, 3, 2, 1, 3, 0, 2, 3, 1, 2, 0, 3, 2,
)
LAST = LEVELS


def units(level):
    if level < LEVELS - 1:
        return [(2 * level, 2**level), (2 * level + 1, -(2**level))]
    if level == LEVELS - 1:
        return [(2 * level, FRAMES // 2)]
    return [(2 * LEVELS - 1, 0)]


def kernel(load, lower, upper, inverse, out, whole, fac, inv, cur, own, gat, fac_sem, z_sem, a_sem, b_sem, far_sem, send_sem, last_sem):
    frame = lax.axis_index("blk")
    row = lax.axis_index("row")
    x, y = row // SIDE, row % SIDE

    def device(shift, dx, dy):
        return ((frame + shift + FRAMES) % FRAMES, ((x + dx) % SIDE) * SIDE + (y + dy) % SIDE)

    first = pltpu.make_async_copy(load.at[0], whole, fac_sem.at[3])
    first.start()
    loads = [
        pltpu.make_async_copy(lower.at[0], fac.at[0], fac_sem.at[0]),
        pltpu.make_async_copy(upper.at[0], fac.at[1], fac_sem.at[1]),
        pltpu.make_async_copy(inverse.at[0], inv, fac_sem.at[2]),
    ]
    for copy in loads:
        copy.start()

    partners = {(0, d, 0) for d in range(1, SIDE)} | {(0, 0, d) for d in range(1, SIDE)}
    for level in range(2):
        for _, shift in units(level):
            partners.add((shift, 0, 0))
            if level in FUSED:
                for d in range(1, SIDE):
                    partners |= {(shift, d, 0), (shift, 0, d)}
    barrier = pltpu.get_barrier_semaphore()
    for partner in sorted(partners):
        pl.semaphore_signal(barrier, inc=1, device_id=device(*partner), device_id_type=MESH)

    def along(level, chunk, index):
        return index if level < LEVELS - 1 else chunk % 2

    def step(turn, d):
        return (d, 0) if turn == 0 else (0, d)

    def line(u, c, turn, at, first=0, count=SIDE):
        if turn == 0:
            return gat.at[u, c, pl.ds(first, count), at]
        return gat.at[u, c, at, pl.ds(first, count)]

    def send(src, dst, sem, recv, to):
        pltpu.make_async_remote_copy(src_ref=src, dst_ref=dst, send_sem=sem, recv_sem=recv, device_id=to, device_id_type=MESH).start()

    def wait(ref, sem):
        pltpu.make_async_copy(ref, ref, sem).wait()

    def begin(level, c):
        value = cur[c].astype(jnp.bfloat16)
        if level == LAST:
            u, _ = units(level)[0]
            turn = along(level, c, 0)
            gat[u, c, x, y] = value
            for d in (2, 1, 3):
                send(gat.at[u, c, x, y], gat.at[u, c, x, y], last_sem.at[c], a_sem.at[u, c], device(0, *step(turn, d)))
            return
        own[level, c] = value
        for i, (u, shift) in enumerate(units(level)):
            turn = along(level, c, i)
            if level in FUSED:
                for d in (2, 1, 3, 0):
                    send(own.at[level, c], gat.at[u, c, x, y], send_sem.at[level, c], a_sem.at[u, c], device(shift, *step(turn, d)))
            else:
                send(own.at[level, c], gat.at[u, c, x, y], send_sem.at[level, c], z_sem.at[u, c], device(shift, 0, 0))

    def spread(level, c):
        for i, (u, _) in enumerate(units(level)):
            turn = along(level, c, i)
            wait(gat.at[u, c, x, y], z_sem.at[u, c])
            for d in (2, 1, 3):
                send(gat.at[u, c, x, y], gat.at[u, c, x, y], send_sem.at[level, c], a_sem.at[u, c], device(0, *step(turn, d)))

    def cross(level, c):
        for i, (u, _) in enumerate(units(level)):
            turn = along(level, c, i)
            at = y if turn == 0 else x
            wait(line(u, c, turn, at, 0, SIDE if level in FUSED else SIDE - 1), a_sem.at[u, c])
            if level in DIRECT:
                for d in (2, 1, 3):
                    block = line(u, c, turn, at)
                    send(block, block, send_sem.at[level, c], far_sem.at[u, c], device(0, *step(1 - turn, d)))
            elif SPLIT:
                for sems, first in ((b_sem, 0), (far_sem, 2)):
                    for d, half in ((1, first), (SIDE - 1, 2 - first)):
                        block = line(u, c, turn, at, half, 2)
                        send(block, block, send_sem.at[level, c], sems.at[u, c], device(0, *step(1 - turn, d)))
            else:
                for d in (1, SIDE - 1):
                    block = line(u, c, turn, at)
                    send(block, block, send_sem.at[level, c], b_sem.at[u, c], device(0, *step(1 - turn, d)))

    def relay(level, c):
        for i, (u, _) in enumerate(units(level)):
            turn = along(level, c, i)
            at = y if turn == 0 else x
            wait(line(u, c, turn, 0 if SPLIT else pl.ds(0, 2)), b_sem.at[u, c])
            for half, d in ((0, 1), (2, SIDE - 1)):
                block = line(u, c, turn, (at + SIDE - d) % SIDE, half, 2)
                send(block, block, send_sem.at[level, c], far_sem.at[u, c], device(0, *step(1 - turn, d)))

    def product(block, u, c):
        return jnp.dot(block, gat[u, c].reshape(SIDE * SIDE * ROWS, WIDTH), preferred_element_type=jnp.float32)

    waited = []

    def close(level, c):
        if not waited:
            waited.append(1)
            for copy in loads:
                copy.wait()
        for i, (u, _) in enumerate(units(level)):
            turn = along(level, c, i)
            blocks = 3 if level in DIRECT else 2 if SPLIT else 1
            wait(line(u, c, turn, pl.ds(0, blocks)), far_sem.at[u, c])
        if level < LEVELS - 1:
            total = cur[c]
            (u, shift), (v, _) = units(level)
            total = total - jnp.where(frame >= shift, product(fac[0, level], u, c), 0.0)
            total = total - jnp.where(frame < FRAMES - shift, product(fac[1, level], v, c), 0.0)
            cur[c] = total
        elif level == LEVELS - 1:
            u, shift = units(level)[0]
            side = 1 - frame // shift
            cur[c] = cur[c] - product(fac[side, level], u, c)
        else:
            u, _ = units(level)[0]
            out[0, :, pl.ds(c * WIDTH, WIDTH)] = product(inv[...], u, c)
        if level < LAST:
            begin(level + 1, c)

    steps = [(begin, 0)]
    for level in range(LEVELS + 1):
        if level not in FUSED and level != LAST:
            steps.append((spread, level))
        steps.append((cross, level))
        if level not in DIRECT:
            steps.append((relay, level))
        steps.append((close, level))

    first.wait()
    for c in range(CHUNKS):
        cur[c] = whole[:, pl.ds(c * WIDTH, WIDTH)]
    pl.semaphore_wait(barrier, len(partners))
    todo = [iter(steps) for _ in range(CHUNKS)]
    for c in ORDER:
        act, level = next(todo[c])
        act(level, c)
    for level in range(LEVELS + 1):
        for c in range(CHUNKS):
            u = units(level)[0][0]
            if level < LEVELS - 1:
                wait(gat.at[pl.ds(u, 2), c], send_sem.at[level, c])
            elif level == LEVELS - 1:
                wait(gat.at[u, c], send_sem.at[level, c])
            else:
                wait(gat.at[u, c, 0, pl.ds(0, SIDE - 1)], last_sem.at[c])
                wait(gat.at[u, c, pl.ds(0, SIDE - 1)], send_sem.at[level, c])


def per_device(load_cases, lower_factor, upper_factor, inverse):
    count = 2 * LEVELS
    return pl.pallas_call(
        kernel,
        out_shape=jax.ShapeDtypeStruct((1, ROWS, CHUNKS * WIDTH), jnp.float32),
        in_specs=[pl.BlockSpec(memory_space=pl.ANY)] * 4,
        out_specs=pl.BlockSpec(memory_space=pltpu.VMEM),
        scratch_shapes=[
            pltpu.VMEM((ROWS, CHUNKS * WIDTH), jnp.float32),
            pltpu.VMEM((2, LEVELS, ROWS, SIDE * SIDE * ROWS), jnp.bfloat16),
            pltpu.VMEM((ROWS, SIDE * SIDE * ROWS), jnp.bfloat16),
            pltpu.VMEM((CHUNKS, ROWS, WIDTH), jnp.float32),
            pltpu.VMEM((LEVELS, CHUNKS, ROWS, WIDTH), jnp.bfloat16),
            pltpu.VMEM((count, CHUNKS, SIDE, SIDE, ROWS, WIDTH), jnp.bfloat16),
            pltpu.SemaphoreType.DMA((4,)),
            pltpu.SemaphoreType.DMA((count, CHUNKS)),
            pltpu.SemaphoreType.DMA((count, CHUNKS)),
            pltpu.SemaphoreType.DMA((count, CHUNKS)),
            pltpu.SemaphoreType.DMA((count, CHUNKS)),
            pltpu.SemaphoreType.DMA((LEVELS + 1, CHUNKS)),
            pltpu.SemaphoreType.DMA((CHUNKS,)),
        ],
        compiler_params=pltpu.CompilerParams(collective_id=0, has_side_effects=True, vmem_limit_bytes=62 * 2**20),
        cost_estimate=pl.CostEstimate(flops=1_660_000_000, bytes_accessed=3_700_000, transcendentals=0),
        name="hull_solve",
    )(load_cases, lower_factor, upper_factor, inverse)


def solution(mesh):
    return jax.shard_map(
        per_device,
        mesh=mesh,
        in_specs=(
            P("blk", "row", None),
            P("blk", None, "row", None),
            P("blk", None, "row", None),
            P("blk", "row", None),
        ),
        out_specs=P("blk", "row", None),
        check_vma=False,
    )
```

```python
import jax
import jax.numpy as jnp
from jax import lax
from jax.experimental import pallas as pl
from jax.experimental.pallas import tpu as pltpu
from jax.sharding import PartitionSpec as P

MESH = pl.DeviceIdType.MESH
LEVELS = 5
FRAMES = 32
SIDE = 4
ROWS = 96
WIDTH = 128
CHUNKS = 4
FUSED = (0, 1)
DIRECT = (4, 5)
SPLIT = True
ORDER = (
    0, 1, 2, 3, 0, 1, 0, 2, 1, 0, 2, 3, 1, 0, 3, 2, 0, 1, 3, 2, 0, 1, 0, 2, 3, 1, 0, 2, 1, 3, 0, 2,
    1, 3, 0, 2, 1, 3, 2, 0, 1, 3, 2, 0, 3, 1, 0, 3, 2, 1, 0, 2, 3, 1, 2, 3, 0, 1, 2, 3, 0, 3, 1, 2,
    1, 3, 2, 0, 3, 1, 0, 2, 1, 3, 2, 0, 3, 2, 1, 3,
)
LAST = LEVELS


def units(level):
    if level < LEVELS - 1:
        return [(2 * level, 2**level), (2 * level + 1, -(2**level))]
    if level == LEVELS - 1:
        return [(2 * level, FRAMES // 2)]
    return [(2 * LEVELS - 1, 0)]


def kernel(load, lower, upper, inverse, out, whole, fac, inv, cur, own, gat, fac_sem, z_sem, a_sem, b_sem, far_sem, send_sem, last_sem):
    frame = lax.axis_index("blk")
    row = lax.axis_index("row")
    x, y = row // SIDE, row % SIDE

    def device(shift, dx, dy):
        return ((frame + shift + FRAMES) % FRAMES, ((x + dx) % SIDE) * SIDE + (y + dy) % SIDE)

    first = pltpu.make_async_copy(load.at[0], whole, fac_sem.at[3])
    first.start()
    loads = [
        pltpu.make_async_copy(lower.at[0], fac.at[0], fac_sem.at[0]),
        pltpu.make_async_copy(upper.at[0], fac.at[1], fac_sem.at[1]),
        pltpu.make_async_copy(inverse.at[0], inv, fac_sem.at[2]),
    ]
    for copy in loads:
        copy.start()

    partners = {(0, d, 0) for d in range(1, SIDE)} | {(0, 0, d) for d in range(1, SIDE)}
    for level in range(2):
        for _, shift in units(level):
            partners.add((shift, 0, 0))
            if level in FUSED:
                for d in range(1, SIDE):
                    partners |= {(shift, d, 0), (shift, 0, d)}
    barrier = pltpu.get_barrier_semaphore()
    for partner in sorted(partners):
        pl.semaphore_signal(barrier, inc=1, device_id=device(*partner), device_id_type=MESH)

    def along(level, chunk, index):
        return index if level < LEVELS - 1 else chunk % 2

    def step(turn, d):
        return (d, 0) if turn == 0 else (0, d)

    def line(u, c, turn, at, first=0, count=SIDE):
        if turn == 0:
            return gat.at[u, c, pl.ds(first, count), at]
        return gat.at[u, c, at, pl.ds(first, count)]

    def send(src, dst, sem, recv, to):
        pltpu.make_async_remote_copy(src_ref=src, dst_ref=dst, send_sem=sem, recv_sem=recv, device_id=to, device_id_type=MESH).start()

    def wait(ref, sem):
        pltpu.make_async_copy(ref, ref, sem).wait()

    def begin(level, c):
        value = cur[c].astype(jnp.bfloat16)
        if level == LAST:
            u, _ = units(level)[0]
            turn = along(level, c, 0)
            gat[u, c, x, y] = value
            for d in (2, 1, 3):
                send(gat.at[u, c, x, y], gat.at[u, c, x, y], last_sem.at[c], a_sem.at[u, c], device(0, *step(turn, d)))
            return
        own[level, c] = value
        for i, (u, shift) in enumerate(units(level)):
            turn = along(level, c, i)
            if level in FUSED:
                for d in (2, 1, 3, 0):
                    send(own.at[level, c], gat.at[u, c, x, y], send_sem.at[level, c], a_sem.at[u, c], device(shift, *step(turn, d)))
            else:
                send(own.at[level, c], gat.at[u, c, x, y], send_sem.at[level, c], z_sem.at[u, c], device(shift, 0, 0))

    def spread(level, c):
        for i, (u, _) in enumerate(units(level)):
            turn = along(level, c, i)
            wait(gat.at[u, c, x, y], z_sem.at[u, c])
            for d in (2, 1, 3):
                send(gat.at[u, c, x, y], gat.at[u, c, x, y], send_sem.at[level, c], a_sem.at[u, c], device(0, *step(turn, d)))

    def cross(level, c):
        for i, (u, _) in enumerate(units(level)):
            turn = along(level, c, i)
            at = y if turn == 0 else x
            wait(line(u, c, turn, at, 0, SIDE if level in FUSED else SIDE - 1), a_sem.at[u, c])
            if level in DIRECT:
                for d in (2, 1, 3):
                    block = line(u, c, turn, at)
                    send(block, block, send_sem.at[level, c], far_sem.at[u, c], device(0, *step(1 - turn, d)))
            elif SPLIT:
                for sems, first in ((b_sem, 0), (far_sem, 2)):
                    for d, half in ((1, first), (SIDE - 1, 2 - first)):
                        block = line(u, c, turn, at, half, 2)
                        send(block, block, send_sem.at[level, c], sems.at[u, c], device(0, *step(1 - turn, d)))
            else:
                for d in (1, SIDE - 1):
                    block = line(u, c, turn, at)
                    send(block, block, send_sem.at[level, c], b_sem.at[u, c], device(0, *step(1 - turn, d)))

    def relay(level, c):
        for i, (u, _) in enumerate(units(level)):
            turn = along(level, c, i)
            at = y if turn == 0 else x
            wait(line(u, c, turn, 0 if SPLIT else pl.ds(0, 2)), b_sem.at[u, c])
            for half, d in ((0, 1), (2, SIDE - 1)):
                block = line(u, c, turn, (at + SIDE - d) % SIDE, half, 2)
                send(block, block, send_sem.at[level, c], far_sem.at[u, c], device(0, *step(1 - turn, d)))

    def product(block, u, c):
        return jnp.dot(block, gat[u, c].reshape(SIDE * SIDE * ROWS, WIDTH), preferred_element_type=jnp.float32)

    waited = []

    def close(level, c):
        if not waited:
            waited.append(1)
            for copy in loads:
                copy.wait()
        for i, (u, _) in enumerate(units(level)):
            turn = along(level, c, i)
            blocks = 3 if level in DIRECT else 2 if SPLIT else 1
            wait(line(u, c, turn, pl.ds(0, blocks)), far_sem.at[u, c])
        if level < LEVELS - 1:
            total = cur[c]
            (u, shift), (v, _) = units(level)
            total = total - jnp.where(frame >= shift, product(fac[0, level], u, c), 0.0)
            total = total - jnp.where(frame < FRAMES - shift, product(fac[1, level], v, c), 0.0)
            cur[c] = total
        elif level == LEVELS - 1:
            u, shift = units(level)[0]
            side = 1 - frame // shift
            cur[c] = cur[c] - product(fac[side, level], u, c)
        else:
            u, _ = units(level)[0]
            out[0, :, pl.ds(c * WIDTH, WIDTH)] = product(inv[...], u, c)
        if level < LAST:
            begin(level + 1, c)

    steps = [(begin, 0)]
    for level in range(LEVELS + 1):
        if level not in FUSED and level != LAST:
            steps.append((spread, level))
        steps.append((cross, level))
        if level not in DIRECT:
            steps.append((relay, level))
        steps.append((close, level))

    first.wait()
    for c in range(CHUNKS):
        cur[c] = whole[:, pl.ds(c * WIDTH, WIDTH)]
    pl.semaphore_wait(barrier, len(partners))
    todo = [iter(steps) for _ in range(CHUNKS)]
    for c in ORDER:
        act, level = next(todo[c])
        act(level, c)
    for level in range(LEVELS + 1):
        for c in range(CHUNKS):
            u = units(level)[0][0]
            if level < LEVELS - 1:
                wait(gat.at[pl.ds(u, 2), c], send_sem.at[level, c])
            elif level == LEVELS - 1:
                wait(gat.at[u, c], send_sem.at[level, c])
            else:
                wait(gat.at[u, c, 0, pl.ds(0, SIDE - 1)], last_sem.at[c])
                wait(gat.at[u, c, pl.ds(0, SIDE - 1)], send_sem.at[level, c])


def per_device(load_cases, lower_factor, upper_factor, inverse):
    count = 2 * LEVELS
    return pl.pallas_call(
        kernel,
        out_shape=jax.ShapeDtypeStruct((1, ROWS, CHUNKS * WIDTH), jnp.float32),
        in_specs=[pl.BlockSpec(memory_space=pl.ANY)] * 4,
        out_specs=pl.BlockSpec(memory_space=pltpu.VMEM),
        scratch_shapes=[
            pltpu.VMEM((ROWS, CHUNKS * WIDTH), jnp.float32),
            pltpu.VMEM((2, LEVELS, ROWS, SIDE * SIDE * ROWS), jnp.bfloat16),
            pltpu.VMEM((ROWS, SIDE * SIDE * ROWS), jnp.bfloat16),
            pltpu.VMEM((CHUNKS, ROWS, WIDTH), jnp.float32),
            pltpu.VMEM((LEVELS, CHUNKS, ROWS, WIDTH), jnp.bfloat16),
            pltpu.VMEM((count, CHUNKS, SIDE, SIDE, ROWS, WIDTH), jnp.bfloat16),
            pltpu.SemaphoreType.DMA((4,)),
            pltpu.SemaphoreType.DMA((count, CHUNKS)),
            pltpu.SemaphoreType.DMA((count, CHUNKS)),
            pltpu.SemaphoreType.DMA((count, CHUNKS)),
            pltpu.SemaphoreType.DMA((count, CHUNKS)),
            pltpu.SemaphoreType.DMA((LEVELS + 1, CHUNKS)),
            pltpu.SemaphoreType.DMA((CHUNKS,)),
        ],
        compiler_params=pltpu.CompilerParams(collective_id=0, has_side_effects=True, vmem_limit_bytes=62 * 2**20),
        cost_estimate=pl.CostEstimate(flops=1_660_000_000, bytes_accessed=3_700_000, transcendentals=0),
        name="hull_solve",
    )(load_cases, lower_factor, upper_factor, inverse)


def solution(mesh):
    return jax.shard_map(
        per_device,
        mesh=mesh,
        in_specs=(
            P("blk", "row", None),
            P("blk", None, "row", None),
            P("blk", None, "row", None),
            P("blk", "row", None),
        ),
        out_specs=P("blk", "row", None),
        check_vma=False,
    )
```

```python
import jax
import jax.numpy as jnp
from jax import lax
from jax.experimental import pallas as pl
from jax.experimental.pallas import tpu as pltpu
from jax.sharding import PartitionSpec as P

MESH = pl.DeviceIdType.MESH
LEVELS = 5
FRAMES = 32
SIDE = 4
ROWS = 96
WIDTH = 128
CHUNKS = 4
FUSED = (0, 1)
DIRECT = (4, 5)
SPLIT = True
ORDER = (
    0, 1, 2, 3, 0, 1, 0, 2, 1, 0, 3, 2, 1, 0, 3, 2, 1, 0, 3, 1, 2, 0, 3, 1, 2, 0, 3, 1, 0, 3, 1, 2,
    0, 3, 1, 2, 0, 3, 1, 2, 3, 0, 2, 1, 3, 0, 2, 1, 0, 3, 1, 2, 0, 3, 1, 2, 3, 2, 0, 3, 1, 2, 0, 1,
    3, 0, 2, 3, 1, 2, 1, 3, 0, 2, 3, 2, 1, 3, 0, 2,
)
LAST = LEVELS


def units(level):
    if level < LEVELS - 1:
        return [(2 * level, 2**level), (2 * level + 1, -(2**level))]
    if level == LEVELS - 1:
        return [(2 * level, FRAMES // 2)]
    return [(2 * LEVELS - 1, 0)]


def kernel(load, lower, upper, inverse, out, whole, fac, inv, cur, own, gat, fac_sem, z_sem, a_sem, b_sem, far_sem, send_sem, last_sem):
    frame = lax.axis_index("blk")
    row = lax.axis_index("row")
    x, y = row // SIDE, row % SIDE

    def device(shift, dx, dy):
        return ((frame + shift + FRAMES) % FRAMES, ((x + dx) % SIDE) * SIDE + (y + dy) % SIDE)

    first = pltpu.make_async_copy(load.at[0], whole, fac_sem.at[3])
    first.start()
    loads = [
        pltpu.make_async_copy(lower.at[0], fac.at[0], fac_sem.at[0]),
        pltpu.make_async_copy(upper.at[0], fac.at[1], fac_sem.at[1]),
        pltpu.make_async_copy(inverse.at[0], inv, fac_sem.at[2]),
    ]
    for copy in loads:
        copy.start()

    partners = {(0, d, 0) for d in range(1, SIDE)} | {(0, 0, d) for d in range(1, SIDE)}
    for level in range(2):
        for _, shift in units(level):
            partners.add((shift, 0, 0))
            if level in FUSED:
                for d in range(1, SIDE):
                    partners |= {(shift, d, 0), (shift, 0, d)}
    barrier = pltpu.get_barrier_semaphore()
    for partner in sorted(partners):
        pl.semaphore_signal(barrier, inc=1, device_id=device(*partner), device_id_type=MESH)

    def along(level, chunk, index):
        return index if level < LEVELS - 1 else chunk % 2

    def step(turn, d):
        return (d, 0) if turn == 0 else (0, d)

    def line(u, c, turn, at, first=0, count=SIDE):
        if turn == 0:
            return gat.at[u, c, pl.ds(first, count), at]
        return gat.at[u, c, at, pl.ds(first, count)]

    def send(src, dst, sem, recv, to):
        pltpu.make_async_remote_copy(src_ref=src, dst_ref=dst, send_sem=sem, recv_sem=recv, device_id=to, device_id_type=MESH).start()

    def wait(ref, sem):
        pltpu.make_async_copy(ref, ref, sem).wait()

    def begin(level, c):
        value = cur[c].astype(jnp.bfloat16)
        if level == LAST:
            u, _ = units(level)[0]
            turn = along(level, c, 0)
            gat[u, c, x, y] = value
            for d in (2, 1, 3):
                send(gat.at[u, c, x, y], gat.at[u, c, x, y], last_sem.at[c], a_sem.at[u, c], device(0, *step(turn, d)))
            return
        own[level, c] = value
        for i, (u, shift) in enumerate(units(level)):
            turn = along(level, c, i)
            if level in FUSED:
                for d in (2, 1, 3, 0):
                    send(own.at[level, c], gat.at[u, c, x, y], send_sem.at[level, c], a_sem.at[u, c], device(shift, *step(turn, d)))
            else:
                send(own.at[level, c], gat.at[u, c, x, y], send_sem.at[level, c], z_sem.at[u, c], device(shift, 0, 0))

    def spread(level, c):
        for i, (u, _) in enumerate(units(level)):
            turn = along(level, c, i)
            wait(gat.at[u, c, x, y], z_sem.at[u, c])
            for d in (2, 1, 3):
                send(gat.at[u, c, x, y], gat.at[u, c, x, y], send_sem.at[level, c], a_sem.at[u, c], device(0, *step(turn, d)))

    def cross(level, c):
        for i, (u, _) in enumerate(units(level)):
            turn = along(level, c, i)
            at = y if turn == 0 else x
            wait(line(u, c, turn, at, 0, SIDE if level in FUSED else SIDE - 1), a_sem.at[u, c])
            if level in DIRECT:
                for d in (2, 1, 3):
                    block = line(u, c, turn, at)
                    send(block, block, send_sem.at[level, c], far_sem.at[u, c], device(0, *step(1 - turn, d)))
            elif SPLIT:
                for sems, first in ((b_sem, 0), (far_sem, 2)):
                    for d, half in ((1, first), (SIDE - 1, 2 - first)):
                        block = line(u, c, turn, at, half, 2)
                        send(block, block, send_sem.at[level, c], sems.at[u, c], device(0, *step(1 - turn, d)))
            else:
                for d in (1, SIDE - 1):
                    block = line(u, c, turn, at)
                    send(block, block, send_sem.at[level, c], b_sem.at[u, c], device(0, *step(1 - turn, d)))

    def relay(level, c):
        for i, (u, _) in enumerate(units(level)):
            turn = along(level, c, i)
            at = y if turn == 0 else x
            wait(line(u, c, turn, 0 if SPLIT else pl.ds(0, 2)), b_sem.at[u, c])
            for half, d in ((0, 1), (2, SIDE - 1)):
                block = line(u, c, turn, (at + SIDE - d) % SIDE, half, 2)
                send(block, block, send_sem.at[level, c], far_sem.at[u, c], device(0, *step(1 - turn, d)))

    def product(block, u, c):
        return jnp.dot(block, gat[u, c].reshape(SIDE * SIDE * ROWS, WIDTH), preferred_element_type=jnp.float32)

    waited = []

    def close(level, c):
        if not waited:
            waited.append(1)
            for copy in loads:
                copy.wait()
        for i, (u, _) in enumerate(units(level)):
            turn = along(level, c, i)
            blocks = 3 if level in DIRECT else 2 if SPLIT else 1
            wait(line(u, c, turn, pl.ds(0, blocks)), far_sem.at[u, c])
        if level < LEVELS - 1:
            total = cur[c]
            (u, shift), (v, _) = units(level)
            total = total - jnp.where(frame >= shift, product(fac[0, level], u, c), 0.0)
            total = total - jnp.where(frame < FRAMES - shift, product(fac[1, level], v, c), 0.0)
            cur[c] = total
        elif level == LEVELS - 1:
            u, shift = units(level)[0]
            side = 1 - frame // shift
            cur[c] = cur[c] - product(fac[side, level], u, c)
        else:
            u, _ = units(level)[0]
            out[0, :, pl.ds(c * WIDTH, WIDTH)] = product(inv[...], u, c)
        if level < LAST:
            begin(level + 1, c)

    steps = [(begin, 0)]
    for level in range(LEVELS + 1):
        if level not in FUSED and level != LAST:
            steps.append((spread, level))
        steps.append((cross, level))
        if level not in DIRECT:
            steps.append((relay, level))
        steps.append((close, level))

    first.wait()
    for c in range(CHUNKS):
        cur[c] = whole[:, pl.ds(c * WIDTH, WIDTH)]
    pl.semaphore_wait(barrier, len(partners))
    todo = [iter(steps) for _ in range(CHUNKS)]
    for c in ORDER:
        act, level = next(todo[c])
        act(level, c)
    for level in range(LEVELS + 1):
        for c in range(CHUNKS):
            u = units(level)[0][0]
            if level < LEVELS - 1:
                wait(gat.at[pl.ds(u, 2), c], send_sem.at[level, c])
            elif level == LEVELS - 1:
                wait(gat.at[u, c], send_sem.at[level, c])
            else:
                wait(gat.at[u, c, 0, pl.ds(0, SIDE - 1)], last_sem.at[c])
                wait(gat.at[u, c, pl.ds(0, SIDE - 1)], send_sem.at[level, c])


def per_device(load_cases, lower_factor, upper_factor, inverse):
    count = 2 * LEVELS
    return pl.pallas_call(
        kernel,
        out_shape=jax.ShapeDtypeStruct((1, ROWS, CHUNKS * WIDTH), jnp.float32),
        in_specs=[pl.BlockSpec(memory_space=pl.ANY)] * 4,
        out_specs=pl.BlockSpec(memory_space=pltpu.VMEM),
        scratch_shapes=[
            pltpu.VMEM((ROWS, CHUNKS * WIDTH), jnp.float32),
            pltpu.VMEM((2, LEVELS, ROWS, SIDE * SIDE * ROWS), jnp.bfloat16),
            pltpu.VMEM((ROWS, SIDE * SIDE * ROWS), jnp.bfloat16),
            pltpu.VMEM((CHUNKS, ROWS, WIDTH), jnp.float32),
            pltpu.VMEM((LEVELS, CHUNKS, ROWS, WIDTH), jnp.bfloat16),
            pltpu.VMEM((count, CHUNKS, SIDE, SIDE, ROWS, WIDTH), jnp.bfloat16),
            pltpu.SemaphoreType.DMA((4,)),
            pltpu.SemaphoreType.DMA((count, CHUNKS)),
            pltpu.SemaphoreType.DMA((count, CHUNKS)),
            pltpu.SemaphoreType.DMA((count, CHUNKS)),
            pltpu.SemaphoreType.DMA((count, CHUNKS)),
            pltpu.SemaphoreType.DMA((LEVELS + 1, CHUNKS)),
            pltpu.SemaphoreType.DMA((CHUNKS,)),
        ],
        compiler_params=pltpu.CompilerParams(collective_id=0, has_side_effects=True, vmem_limit_bytes=62 * 2**20),
        cost_estimate=pl.CostEstimate(flops=1_660_000_000, bytes_accessed=3_700_000, transcendentals=0),
        name="hull_solve",
    )(load_cases, lower_factor, upper_factor, inverse)


def solution(mesh):
    return jax.shard_map(
        per_device,
        mesh=mesh,
        in_specs=(
            P("blk", "row", None),
            P("blk", None, "row", None),
            P("blk", None, "row", None),
            P("blk", "row", None),
        ),
        out_specs=P("blk", "row", None),
        check_vma=False,
    )
```

```python
import jax
import jax.numpy as jnp
from jax import lax
from jax.experimental import pallas as pl
from jax.experimental.pallas import tpu as pltpu
from jax.sharding import PartitionSpec as P

MESH = pl.DeviceIdType.MESH
LEVELS = 5
FRAMES = 32
SIDE = 4
ROWS = 96
WIDTH = 128
CHUNKS = 4
FUSED = (0, 1)
DIRECT = (4, 5)
SPLIT = True
ORDER = (
    1, 3, 0, 2, 1, 0, 1, 2, 0, 1, 3, 2, 0, 3, 1, 2, 0, 1, 3, 0, 2, 1, 3, 0, 2, 1, 3, 0, 2, 1, 3, 0,
    1, 2, 0, 3, 1, 2, 0, 3, 2, 1, 3, 0, 2, 1, 3, 0, 1, 2, 0, 3, 1, 2, 0, 3, 2, 3, 1, 2, 0, 3, 1, 0,
    2, 1, 3, 2, 0, 3, 0, 2, 1, 3, 2, 0, 3, 1, 2, 3,
)
LAST = LEVELS


def units(level):
    if level < LEVELS - 1:
        return [(2 * level, 2**level), (2 * level + 1, -(2**level))]
    if level == LEVELS - 1:
        return [(2 * level, FRAMES // 2)]
    return [(2 * LEVELS - 1, 0)]


def kernel(load, lower, upper, inverse, out, whole, fac, inv, cur, own, gat, fac_sem, z_sem, a_sem, b_sem, far_sem, send_sem, last_sem):
    frame = lax.axis_index("blk")
    row = lax.axis_index("row")
    x, y = row // SIDE, row % SIDE

    def device(shift, dx, dy):
        return ((frame + shift + FRAMES) % FRAMES, ((x + dx) % SIDE) * SIDE + (y + dy) % SIDE)

    first = pltpu.make_async_copy(load.at[0], whole, fac_sem.at[3])
    first.start()
    loads = [
        pltpu.make_async_copy(lower.at[0], fac.at[0], fac_sem.at[0]),
        pltpu.make_async_copy(upper.at[0], fac.at[1], fac_sem.at[1]),
        pltpu.make_async_copy(inverse.at[0], inv, fac_sem.at[2]),
    ]
    for copy in loads:
        copy.start()

    partners = {(0, d, 0) for d in range(1, SIDE)} | {(0, 0, d) for d in range(1, SIDE)}
    for level in range(2):
        for _, shift in units(level):
            partners.add((shift, 0, 0))
            if level in FUSED:
                for d in range(1, SIDE):
                    partners |= {(shift, d, 0), (shift, 0, d)}
    barrier = pltpu.get_barrier_semaphore()
    for partner in sorted(partners):
        pl.semaphore_signal(barrier, inc=1, device_id=device(*partner), device_id_type=MESH)

    def along(level, chunk, index):
        return index if level < LEVELS - 1 else chunk % 2

    def step(turn, d):
        return (d, 0) if turn == 0 else (0, d)

    def line(u, c, turn, at, first=0, count=SIDE):
        if turn == 0:
            return gat.at[u, c, pl.ds(first, count), at]
        return gat.at[u, c, at, pl.ds(first, count)]

    def send(src, dst, sem, recv, to):
        pltpu.make_async_remote_copy(src_ref=src, dst_ref=dst, send_sem=sem, recv_sem=recv, device_id=to, device_id_type=MESH).start()

    def wait(ref, sem):
        pltpu.make_async_copy(ref, ref, sem).wait()

    def begin(level, c):
        value = cur[c].astype(jnp.bfloat16)
        if level == LAST:
            u, _ = units(level)[0]
            turn = along(level, c, 0)
            gat[u, c, x, y] = value
            for d in (2, 1, 3):
                send(gat.at[u, c, x, y], gat.at[u, c, x, y], last_sem.at[c], a_sem.at[u, c], device(0, *step(turn, d)))
            return
        if level > 0:
            own[level, c] = value
        for i, (u, shift) in enumerate(units(level)):
            turn = along(level, c, i)
            if level in FUSED:
                for d in (2, 1, 3, 0):
                    send(own.at[level, c], gat.at[u, c, x, y], send_sem.at[level, c], a_sem.at[u, c], device(shift, *step(turn, d)))
            else:
                send(own.at[level, c], gat.at[u, c, x, y], send_sem.at[level, c], z_sem.at[u, c], device(shift, 0, 0))

    def spread(level, c):
        for i, (u, _) in enumerate(units(level)):
            turn = along(level, c, i)
            wait(gat.at[u, c, x, y], z_sem.at[u, c])
            for d in (2, 1, 3):
                send(gat.at[u, c, x, y], gat.at[u, c, x, y], send_sem.at[level, c], a_sem.at[u, c], device(0, *step(turn, d)))

    def cross(level, c):
        for i, (u, _) in enumerate(units(level)):
            turn = along(level, c, i)
            at = y if turn == 0 else x
            wait(line(u, c, turn, at, 0, SIDE if level in FUSED else SIDE - 1), a_sem.at[u, c])
            if level in DIRECT:
                for d in (2, 1, 3):
                    block = line(u, c, turn, at)
                    send(block, block, send_sem.at[level, c], far_sem.at[u, c], device(0, *step(1 - turn, d)))
            elif SPLIT:
                for sems, first in ((b_sem, 0), (far_sem, 2)):
                    for d, half in ((1, first), (SIDE - 1, 2 - first)):
                        block = line(u, c, turn, at, half, 2)
                        send(block, block, send_sem.at[level, c], sems.at[u, c], device(0, *step(1 - turn, d)))
            else:
                for d in (1, SIDE - 1):
                    block = line(u, c, turn, at)
                    send(block, block, send_sem.at[level, c], b_sem.at[u, c], device(0, *step(1 - turn, d)))

    def relay(level, c):
        for i, (u, _) in enumerate(units(level)):
            turn = along(level, c, i)
            at = y if turn == 0 else x
            wait(line(u, c, turn, 0 if SPLIT else pl.ds(0, 2)), b_sem.at[u, c])
            for half, d in ((0, 1), (2, SIDE - 1)):
                block = line(u, c, turn, (at + SIDE - d) % SIDE, half, 2)
                send(block, block, send_sem.at[level, c], far_sem.at[u, c], device(0, *step(1 - turn, d)))

    def product(block, u, c):
        return jnp.dot(block, gat[u, c].reshape(SIDE * SIDE * ROWS, WIDTH), preferred_element_type=jnp.float32)

    waited = []

    def close(level, c):
        if not waited:
            waited.append(1)
            for copy in loads:
                copy.wait()
        for i, (u, _) in enumerate(units(level)):
            turn = along(level, c, i)
            blocks = 3 if level in DIRECT else 2 if SPLIT else 1
            wait(line(u, c, turn, pl.ds(0, blocks)), far_sem.at[u, c])
        if level < LEVELS - 1:
            total = cur[c]
            (u, shift), (v, _) = units(level)
            total = total - jnp.where(frame >= shift, product(fac[0, level], u, c), 0.0)
            total = total - jnp.where(frame < FRAMES - shift, product(fac[1, level], v, c), 0.0)
            cur[c] = total
        elif level == LEVELS - 1:
            u, shift = units(level)[0]
            side = 1 - frame // shift
            cur[c] = cur[c] - product(fac[side, level], u, c)
        else:
            u, _ = units(level)[0]
            out[0, :, pl.ds(c * WIDTH, WIDTH)] = product(inv[...], u, c)
        if level < LAST:
            begin(level + 1, c)

    steps = [(begin, 0)]
    for level in range(LEVELS + 1):
        if level not in FUSED and level != LAST:
            steps.append((spread, level))
        steps.append((cross, level))
        if level not in DIRECT:
            steps.append((relay, level))
        steps.append((close, level))

    first.wait()
    for c in range(CHUNKS):
        cur[c] = whole[:, pl.ds(c * WIDTH, WIDTH)]
        own[0, c] = cur[c].astype(jnp.bfloat16)
    pl.semaphore_wait(barrier, len(partners))
    todo = [iter(steps) for _ in range(CHUNKS)]
    for c in ORDER:
        act, level = next(todo[c])
        act(level, c)
    for level in range(LEVELS + 1):
        for c in range(CHUNKS):
            u = units(level)[0][0]
            if level < LEVELS - 1:
                wait(gat.at[pl.ds(u, 2), c], send_sem.at[level, c])
            elif level == LEVELS - 1:
                wait(gat.at[u, c], send_sem.at[level, c])
            else:
                wait(gat.at[u, c, 0, pl.ds(0, SIDE - 1)], last_sem.at[c])
                wait(gat.at[u, c, pl.ds(0, SIDE - 1)], send_sem.at[level, c])


def per_device(load_cases, lower_factor, upper_factor, inverse):
    count = 2 * LEVELS
    return pl.pallas_call(
        kernel,
        out_shape=jax.ShapeDtypeStruct((1, ROWS, CHUNKS * WIDTH), jnp.float32),
        in_specs=[pl.BlockSpec(memory_space=pl.ANY)] * 4,
        out_specs=pl.BlockSpec(memory_space=pltpu.VMEM),
        scratch_shapes=[
            pltpu.VMEM((ROWS, CHUNKS * WIDTH), jnp.float32),
            pltpu.VMEM((2, LEVELS, ROWS, SIDE * SIDE * ROWS), jnp.bfloat16),
            pltpu.VMEM((ROWS, SIDE * SIDE * ROWS), jnp.bfloat16),
            pltpu.VMEM((CHUNKS, ROWS, WIDTH), jnp.float32),
            pltpu.VMEM((LEVELS, CHUNKS, ROWS, WIDTH), jnp.bfloat16),
            pltpu.VMEM((count, CHUNKS, SIDE, SIDE, ROWS, WIDTH), jnp.bfloat16),
            pltpu.SemaphoreType.DMA((4,)),
            pltpu.SemaphoreType.DMA((count, CHUNKS)),
            pltpu.SemaphoreType.DMA((count, CHUNKS)),
            pltpu.SemaphoreType.DMA((count, CHUNKS)),
            pltpu.SemaphoreType.DMA((count, CHUNKS)),
            pltpu.SemaphoreType.DMA((LEVELS + 1, CHUNKS)),
            pltpu.SemaphoreType.DMA((CHUNKS,)),
        ],
        compiler_params=pltpu.CompilerParams(collective_id=0, has_side_effects=True, vmem_limit_bytes=62 * 2**20),
        cost_estimate=pl.CostEstimate(flops=1_660_000_000, bytes_accessed=3_700_000, transcendentals=0),
        name="hull_solve",
    )(load_cases, lower_factor, upper_factor, inverse)


def solution(mesh):
    return jax.shard_map(
        per_device,
        mesh=mesh,
        in_specs=(
            P("blk", "row", None),
            P("blk", None, "row", None),
            P("blk", None, "row", None),
            P("blk", "row", None),
        ),
        out_specs=P("blk", "row", None),
        check_vma=False,
    )
```
